32 devices in a mesh: groups: 2 (over x), vocab: 16 (over z, y, core).
Axes of the slice: x: 2, y: 2, z: 4, core: 2. Of those that a mesh axis runs over, the one named last changes fastest.
Arguments:
- hidden: bfloat16 [4096, 5376], P(('groups', 'vocab')), parts along dimension 0, may hold values from -1.5 to 1.5
- weight: bfloat16 [16384, 5376], P('vocab'), may hold values from -0.3125 to 0.3125
- lse: float32 [4096], P('groups'), parts along dimension 0, may hold values from 4 to 6.5
- loss_grad: float32 [4096], P('groups'), parts along dimension 0, may hold values from 0.5 to 8
- labels: int32 [4096], P('groups'), parts along dimension 0, may hold values from 0 to 16383, as said below
- kept_blocks: int32 [32, 3], P(('groups', 'vocab')), parts along dimension 0, may hold values from 0 to 15, as said below
- kept_count: int32 [32], P(('groups', 'vocab')), parts along dimension 0, may hold values from 1 to 3, as said below
Outputs:
- grad_hidden: bfloat16 [4096, 5376], P(('groups', 'vocab')), parts along dimension 0
- grad_weight: bfloat16 [32768, 5376], P(('groups', 'vocab')), parts along dimension 0
The draws below stay inside these ranges and needn't reach their ends.
There are 2 independent parts, one for each index of `groups`. The reference program is written for one: setup_inputs(seed, part) draws one part's arguments, and reference() takes and returns one part's arrays. A program takes and returns all parts, laid end to end along the dimension named above; an argument that names none is the same for every part. Nothing has to cross between parts.
Inputs may be any that keep to these rules, and one draw needn't show every extreme that they name: `kept_blocks`: row block indices; a shard's list holds distinct row blocks, its first kept_count entries are kept and the rest are other row blocks that are not kept; every row block is kept by at least one shard. `kept_count`: some shard's count is 3 in every draw. `labels`: each token's label is an entry of a shard that keeps the token's row block.
All inputs are finite; a program needn't handle non-finite values.
Results may differ from the reference program's by a relative error of at most 0.006.
Values may be sent and summed in bfloat16 or wider, within the bound.
A program may use at most 192 MiB of HBM per device.

```python
import math
import jax
import jax.numpy as jnp
from jax import lax

D = 5376
VOC_DEV = 1024
RB = 128
TOK_DEV = 128
TOKENS = 2048
VOCAB = 16384
RBLKS = 16
SUB = 8
KMAX = 3
N_VOCAB = 16


def kept_tables(key):
    base_count = TOK_DEV // RB
    order_all = jax.random.permutation(jax.random.fold_in(key, 11), RBLKS).astype(jnp.int32)
    base = order_all.reshape(N_VOCAB, base_count)
    positions = jnp.arange(RBLKS, dtype=jnp.int32)
    base_mask = jnp.any(base[:, :, None] == positions[None, None, :], axis=1)
    scores = jax.random.randint(jax.random.fold_in(key, 12), (N_VOCAB, RBLKS), 0, 1 << 20) * RBLKS + positions[None, :]
    scores = jnp.where(base_mask, positions[None, :] - RBLKS, scores)
    ranked = jnp.argsort(scores, axis=1, stable=True).astype(jnp.int32)
    lists = ranked[:, :KMAX]
    extra_top = KMAX - base_count
    extra = jax.random.randint(jax.random.fold_in(key, 13), (N_VOCAB,), 0, extra_top + 1)
    busiest = jax.random.randint(jax.random.fold_in(key, 14), (), 0, N_VOCAB)
    extra = jnp.where(jnp.arange(N_VOCAB, dtype=jnp.int32) == busiest, KMAX - base_count, extra)
    counts = (base_count + extra).astype(jnp.int32)
    return (lists, counts)


def draw_kept_blocks(key, part):
    lists, counts = kept_tables(key)
    return lists


def draw_kept_count(key, part):
    lists, counts = kept_tables(key)
    return counts


def draw_labels(key, part):
    lists, counts = kept_tables(key)
    key = jax.random.fold_in(key, 3)
    valid = jnp.arange(KMAX, dtype=jnp.int32)[None, :] < counts[:, None]
    positions = jnp.arange(RBLKS, dtype=jnp.int32)
    keeps = jnp.any((lists[:, :, None] == positions[None, None, :]) & valid[:, :, None], axis=1)
    tokens = jnp.arange(TOKENS, dtype=jnp.int32)
    token_block = tokens % TOK_DEV // SUB
    keeper = keeps[:, token_block]
    shard_ids = jnp.arange(N_VOCAB, dtype=jnp.int32)
    scores = jax.random.randint(jax.random.fold_in(key, 21), (N_VOCAB, TOKENS), 1, 1 << 20) * N_VOCAB + shard_ids[:, None]
    scores = jnp.where(keeper, scores, -1)
    owner = jnp.argmax(scores, axis=0).astype(jnp.int32)
    within = jax.random.randint(jax.random.fold_in(key, 22), (TOKENS,), 0, VOC_DEV)
    return (owner * VOC_DEV + within).astype(jnp.int32)


def levels(rng, dims, cuts, least, high):
    gain, own = 1.0, jax.random.fold_in(rng, 6)
    for axis_at, blocks in cuts:
        draws = jnp.exp(jax.random.uniform(jax.random.fold_in(own, axis_at), (blocks,), jnp.float32, least / len(cuts), high / len(cuts)))
        gain = gain * jnp.repeat(draws, dims[axis_at] // blocks).reshape([-1 if axis == axis_at else 1 for axis in range(len(dims))])
    return gain


def normal_values(key, extent, deviation, bound, shards=(), kind=jnp.bfloat16):
    level = levels(key, extent, shards, -0.22, 0.18) if shards else 1.0
    drawn = jax.random.normal(key, extent, jnp.float32) * deviation * level
    return jnp.minimum(jnp.maximum(drawn, -bound), bound).astype(kind)


def setup_inputs(seed: int = 0, part: int = 0) -> dict:
    key_list = jax.random.split(jax.random.key(seed), 8)
    own_keys = jax.random.split(jax.random.fold_in(key_list[7], part), 8)
    hidden = normal_values(own_keys[0], (TOKENS, D), 0.25, 1.5, ((0, 16),))
    weight = normal_values(key_list[1], (VOCAB, D), (D // 16) ** -0.5, 0.3125, ((0, 16),))
    lse = jnp.clip(jax.random.uniform(own_keys[2], (TOKENS,), jnp.float32, 4.0, 6.5), 4.0, 6.5)
    loss_grad = jnp.clip(jnp.exp(jax.random.uniform(own_keys[3], (TOKENS,), jnp.float32, math.log(0.5), math.log(8.0))), 0.5, 8.0)
    labels = draw_labels(jax.random.fold_in(jax.random.fold_in(key_list[7], part), 71), part)
    kept_blocks = draw_kept_blocks(jax.random.fold_in(jax.random.fold_in(key_list[7], part), 71), part)
    kept_count = draw_kept_count(jax.random.fold_in(jax.random.fold_in(key_list[7], part), 71), part)
    return dict(hidden=hidden, weight=weight, lse=lse, loss_grad=loss_grad, labels=labels, kept_blocks=kept_blocks, kept_count=kept_count)


def reference(hidden, weight, lse, loss_grad, labels, kept_blocks, kept_count):
    hidden_tab = hidden.reshape(N_VOCAB, RBLKS, SUB, D)
    label_tab = labels.reshape(N_VOCAB, RBLKS, SUB)
    lse_tab = lse.reshape(N_VOCAB, RBLKS, SUB)
    scale_tab = loss_grad.reshape(N_VOCAB, RBLKS, SUB)
    weight_tab = weight.reshape(N_VOCAB, VOC_DEV, D)

    def per_shard(grad_acc, inputs):
        shard_id, shard_weight, shard_list, shard_count = inputs
        vocab_ids = shard_id * VOC_DEV + jnp.arange(VOC_DEV, dtype=jnp.int32)

        def slot_step(slot_index, carried):
            grad_w, grad_h = carried
            row_block = shard_list[slot_index].astype(jnp.int32)
            block_rows = lax.dynamic_index_in_dim(hidden_tab, row_block, 1, keepdims=False).reshape(RB, D)
            picked_labels = lax.dynamic_index_in_dim(label_tab, row_block, 1, keepdims=False).reshape(RB)
            picked_lse = lax.dynamic_index_in_dim(lse_tab, row_block, 1, keepdims=False).reshape(RB)
            picked_scale = lax.dynamic_index_in_dim(scale_tab, row_block, 1, keepdims=False).reshape(RB)
            logits = jnp.dot(block_rows, shard_weight.T, preferred_element_type=jnp.float32)
            onehot = (picked_labels[:, None] == vocab_ids[None, :]).astype(jnp.float32)
            block_grad = (picked_scale[:, None] * (jnp.exp(logits - picked_lse[:, None]) - onehot)).astype(jnp.bfloat16)
            hidden_part = jnp.dot(block_grad, shard_weight, preferred_element_type=jnp.float32).astype(jnp.bfloat16)
            grad_w = grad_w + jnp.dot(block_grad.T, block_rows, preferred_element_type=jnp.float32)
            current = lax.dynamic_slice_in_dim(grad_h, row_block, 1, 1)
            current = current + hidden_part.reshape(N_VOCAB, 1, SUB, D).astype(jnp.float32)
            grad_h = lax.dynamic_update_slice_in_dim(grad_h, current, row_block, 1)
            return grad_w, grad_h

        start = (jnp.zeros((VOC_DEV, D), jnp.float32), grad_acc)
        grad_w, grad_acc = lax.fori_loop(0, shard_count, slot_step, start)
        return grad_acc, grad_w.astype(jnp.bfloat16)

    initial = jnp.zeros((N_VOCAB, RBLKS, SUB, D), jnp.float32)
    shard_ids = jnp.arange(N_VOCAB, dtype=jnp.int32)
    grad_h, grad_ws = lax.scan(per_shard, initial, (shard_ids, weight_tab, kept_blocks, kept_count))
    return grad_h.reshape(TOKENS, D).astype(jnp.bfloat16), grad_ws.reshape(VOCAB, D)
```

```python
import functools

import jax
import jax.numpy as jnp
from jax import lax
from jax.experimental import pallas as pl
from jax.experimental.pallas import tpu as pltpu
from jax.sharding import PartitionSpec as P

RB = 128
MESH = pl.DeviceIdType.MESH
VMEM_CAP = 60 * 1024 * 1024


def exchange_kernel(
    n, rows, chunks, sw,
    hid, w_hbm, lists, lab, lse, scl,
    gh, g_ref, x_ref,
    w, gw, lists_buf, out_buf, in_buf, hbuf, ret, gret, gsum, part, sel, logits,
    w_sem, l_send, l_recv, s1_send, s1_recv, s2_send, in_recv,
    r_send, ret_recv, gret_recv, gs_send, part_recv,
):
    half, quarter = n // 2, n // 4
    cw = 2 * sw
    me = lax.axis_index("vocab")
    q = lax.rem(me, quarter)
    side = lax.div(me, half)
    hb = side * half
    ob = half - hb
    ml = me - hb
    plane = lax.div(ml, quarter)
    gate_base = quarter + side * quarter
    gate_target = half - side * quarter + q
    is_gate = plane == 1 - side
    f32, bf16 = jnp.float32, jnp.bfloat16

    def remote(src, dst, send, recv, to):
        return pltpu.make_async_remote_copy(
            src_ref=src, dst_ref=dst, send_sem=send, recv_sem=recv,
            device_id={"vocab": to}, device_id_type=MESH,
        )

    def wait_for(ref, sem):
        pltpu.make_async_copy(ref, ref, sem).wait()

    def cols(c):
        return pl.ds(pl.multiple_of(c * cw, 128), cw)

    def subs(c, a):
        return pl.ds(pl.multiple_of(c * cw + a * sw, 128), sw)

    def peer(dd):
        return hb + lax.rem(ml + 1 + dd, half)

    def source(i):
        return ob + i * quarter + q

    barrier = pltpu.get_barrier_semaphore()

    @pl.loop(1, n)
    def _(d):
        pl.semaphore_signal(
            barrier, inc=1, device_id={"vocab": lax.rem(me + d, n)}, device_id_type=MESH
        )

    pl.semaphore_wait(barrier, n - 1)

    def relay_copy(c):
        return remote(
            hid.at[:, cols(c)], gw.at[plane, c], s1_send.at[c], s1_recv.at[plane, c], gate_target
        )

    @pl.loop(0, half - 1)
    def _(dd):
        remote(lists, lists_buf.at[half - 2 - dd], l_send, l_recv, peer(dd)).start()

    pltpu.make_async_copy(lists, lists_buf.at[half - 1], l_recv).start()
    relay_copy(0).start()
    relay_copy(1).start()
    weight_copy = pltpu.make_async_copy(w_hbm, w, w_sem)
    weight_copy.start()
    wait_for(lists_buf, l_recv)
    wanted = lists_buf[...].reshape(half * rows, lists.shape[1])
    lane = lax.broadcasted_iota(jnp.int32, wanted.shape, 1)
    sel[...] = (wanted == lane).astype(f32).astype(bf16)

    def pack(value, count):
        v = value.reshape(count, rows, cw)
        return jnp.concatenate([v[:, :, :sw], v[:, :, sw:]], axis=1).astype(bf16)

    def unpack(value, count):
        v = value.astype(f32)
        parts = [v[:, a * rows : (a + 1) * rows, :].reshape(count * rows, sw) for a in range(2)]
        return [p.astype(bf16) for p in parts]

    def send_rows(c, kind, block, owner):
        picked = jnp.dot(sel[...], block, preferred_element_type=f32)
        out_buf[c, kind] = pack(picked, half)

        @pl.loop(0, half - 1)
        def _(dd):
            remote(
                out_buf.at[c, kind, dd], in_buf.at[c, owner],
                s2_send.at[c, kind], in_recv.at[c], peer(dd),
            ).start()

        pltpu.make_async_copy(
            out_buf.at[c, kind, half - 1], in_buf.at[c, owner], in_recv.at[c]
        ).start()

    def logits_step(c):
        wait_for(in_buf.at[c], in_recv.at[c])
        x0, x1 = unpack(in_buf[c], n)
        x_ref[:, subs(c, 0)] = x0
        x_ref[:, subs(c, 1)] = x1
        dims = (((1,), (1,)), ((), ()))
        logits[...] += lax.dot_general(
            x_ref[:, cols(c)], w[:, cols(c)], dims, preferred_element_type=f32
        )

    logits[...] = jnp.zeros_like(logits)
    weight_copy.wait()
    lag = 2

    @pl.loop(0, chunks + lag)
    def _(c):
        @pl.when(c + 2 < chunks)
        def _():
            relay_copy(c + 2).start()

        @pl.when(c < chunks)
        def _():
            send_rows(c, 0, hid[:, cols(c)], me)

            @pl.when(is_gate)
            def _():
                @pl.loop(0, 2)
                def _(i):
                    wait_for(gw.at[i, c], s1_recv.at[i, c])
                    send_rows(c, 1 + i, gw[i, c], source(i))

        @pl.when(c >= lag)
        def _():
            logits_step(c - lag)

    ids = lax.broadcasted_iota(jnp.int32, logits.shape, 1) + me * logits.shape[1]
    onehot = (lab[...] == ids).astype(f32)
    grad = scl[...] * (jnp.exp(logits[...] - lse[...]) - onehot)
    g_ref[...] = jnp.where(scl[...] != 0, grad, 0.0).astype(bf16)

    def gather_sum(values):
        y = jnp.concatenate(unpack(values, half), axis=1)
        return lax.dot_general(
            sel[...], y, (((0,), (0,)), ((), ())), preferred_element_type=f32
        )

    @pl.loop(0, chunks + 2 * lag)
    def _(c):
        @pl.when(c < chunks)
        def _():
            hp = jnp.dot(g_ref[...], w[:, cols(c)], preferred_element_type=f32)
            hbuf[c] = pack(hp, n)

            def far(i, off):
                qq = lax.rem(q + off, quarter)
                gate = gate_base + qq
                d = lax.rem(ml - (gate - hb) - 1 + half, half)
                return remote(
                    hbuf.at[c, ob + i * quarter + qq], gret.at[c, i, d],
                    r_send.at[c], gret_recv.at[c, i], gate,
                )

            @pl.loop(0, 2)
            def _(i):
                @pl.loop(1, quarter)
                def _(off):
                    far(i, off).start()

                @pl.when(is_gate)
                def _():
                    pltpu.make_async_copy(
                        hbuf.at[c, source(i)], gret.at[c, i, half - 1], gret_recv.at[c, i]
                    ).start()

                @pl.when(jnp.logical_not(is_gate))
                def _():
                    far(i, 0).start()

            @pl.loop(0, half - 1)
            def _(dd):
                remote(
                    hbuf.at[c, peer(dd)], ret.at[c, half - 2 - dd],
                    r_send.at[c], ret_recv.at[c], peer(dd),
                ).start()

            pltpu.make_async_copy(hbuf.at[c, me], ret.at[c, half - 1], ret_recv.at[c]).start()

        @pl.when((c >= lag) & (c < chunks + lag) & is_gate)
        def _():
            k = c - lag

            @pl.loop(0, 2)
            def _(i):
                wait_for(gret.at[k, i], gret_recv.at[k, i])
                gsum[k, i] = gather_sum(gret[k, i]).astype(bf16)
                remote(
                    gsum.at[k, i], part.at[k], gs_send.at[k, i], part_recv.at[k], source(i)
                ).start()

        @pl.when(c >= 2 * lag)
        def _():
            k = c - 2 * lag
            wait_for(ret.at[k], ret_recv.at[k])
            near = gather_sum(ret[k])
            wait_for(part.at[k], part_recv.at[k])
            gh[:, cols(k)] = (near + part[k].astype(f32)).astype(bf16)

    wait_for(lists_buf.at[pl.ds(0, half - 1)], l_send)

    @pl.loop(0, chunks)
    def _(c):
        wait_for(gw.at[0, c], s1_send.at[c])
        wait_for(out_buf.at[c, 0, pl.ds(0, half - 1)], s2_send.at[c, 0])

        @pl.when(is_gate)
        def _():
            @pl.loop(0, 2)
            def _(i):
                wait_for(out_buf.at[c, 1 + i, pl.ds(0, half - 1)], s2_send.at[c, 1 + i])
                wait_for(gsum.at[c, i], gs_send.at[c, i])

            wait_for(hbuf.at[c, pl.ds(0, half + 2 * quarter - 3)], r_send.at[c])

        @pl.when(jnp.logical_not(is_gate))
        def _():
            wait_for(hbuf.at[c, pl.ds(0, half + 2 * quarter - 1)], r_send.at[c])


def scratch_of(n, rows, chunks, sw, toks, voc, width):
    half = n // 2
    bf16 = jnp.bfloat16
    dma = pltpu.SemaphoreType.DMA
    return [
        pltpu.VMEM((voc, width), bf16),
        pltpu.VMEM((2, chunks, toks, 2 * sw), bf16),
        pltpu.VMEM((half, rows, toks), jnp.int32),
        pltpu.VMEM((chunks, 3, half, 2 * rows, sw), bf16),
        pltpu.VMEM((chunks, n, 2 * rows, sw), bf16),
        pltpu.VMEM((chunks, n, 2 * rows, sw), bf16),
        pltpu.VMEM((chunks, half, 2 * rows, sw), bf16),
        pltpu.VMEM((chunks, 2, half, 2 * rows, sw), bf16),
        pltpu.VMEM((chunks, 2, toks, 2 * sw), bf16),
        pltpu.VMEM((chunks, toks, 2 * sw), bf16),
        pltpu.VMEM((half * rows, toks), bf16),
        pltpu.VMEM((n * rows, voc), jnp.float32),
        dma, dma, dma,
        dma((chunks,)), dma((2, chunks)), dma((chunks, 3)), dma((chunks,)),
        dma((chunks,)), dma((chunks,)), dma((chunks, 2)), dma((chunks, 2)), dma((chunks,)),
    ]


def plan(n, tok_rows, voc, width, slots):
    rows = slots * (RB // n)
    if n % 4 or rows % 8 or tok_rows != 128 or width % 256:
        return None
    pairs = width // 256
    chunks = min([c for c in range(1, pairs + 1) if pairs % c == 0], key=lambda c: abs(c - 7))
    need = 2 * voc * width + 4 * n * rows * voc + 2 * n * rows * voc
    need += 2 * width * (n * rows * 6 + tok_rows * 7)
    if need > VMEM_CAP - 3 * 1024 * 1024:
        return None
    return rows, chunks, width // chunks // 2


def per_device(hidden, weight, lse, loss_grad, labels, kept_blocks, kept_count):
    n = lax.axis_size("vocab")
    tok_rows, width = hidden.shape
    voc = weight.shape[0]
    slots = kept_blocks.shape[1]
    planned = plan(n, tok_rows, voc, width, slots)
    if planned is None:
        return by_slots(hidden, weight, lse, loss_grad, labels, kept_blocks, kept_count)
    rows, chunks, sw = planned
    sub = RB // n
    nblocks = tok_rows // sub
    own = kept_blocks[0]
    lists = own[:, None] * sub + jnp.arange(sub, dtype=jnp.int32)[None, :]
    lists = jnp.broadcast_to(lists.reshape(rows, 1), (rows, tok_rows))

    def pick(table):
        return table.reshape(n, nblocks, sub)[:, own, :].reshape(n * rows, 1)

    kept = (jnp.arange(slots, dtype=jnp.int32) < kept_count[0]).astype(jnp.float32)
    scale = loss_grad.reshape(n, nblocks, sub)[:, own, :] * kept[None, :, None]
    vmem = pl.BlockSpec(memory_space=pltpu.VMEM)
    grad_h, g, x = pl.pallas_call(
        functools.partial(exchange_kernel, n, rows, chunks, sw),
        out_shape=(
            jax.ShapeDtypeStruct((tok_rows, width), jnp.bfloat16),
            jax.ShapeDtypeStruct((n * rows, voc), jnp.bfloat16),
            jax.ShapeDtypeStruct((n * rows, width), jnp.bfloat16),
        ),
        in_specs=[vmem, pl.BlockSpec(memory_space=pl.ANY), vmem, vmem, vmem, vmem],
        out_specs=(vmem, vmem, vmem),
        scratch_shapes=scratch_of(n, rows, chunks, sw, tok_rows, voc, width),
        compiler_params=pltpu.CompilerParams(
            collective_id=0, has_side_effects=True, vmem_limit_bytes=VMEM_CAP
        ),
        name="exchange",
    )(hidden, weight, lists, pick(labels), pick(lse), scale.reshape(n * rows, 1))
    grad_w = lax.dot_general(
        g, x, (((0,), (0,)), ((), ())), preferred_element_type=jnp.float32
    )
    return grad_h, grad_w.astype(jnp.bfloat16)


def by_slots(hidden, weight, lse, loss_grad, labels, kept_blocks, kept_count):
    shards = lax.axis_size("vocab")
    my_index = lax.axis_index("vocab")
    tok_rows, feat_width = hidden.shape
    voc_rows = weight.shape[0]
    slot_count = kept_blocks.shape[1]
    sub_rows = RB // shards
    nblocks = tok_rows // sub_rows
    local_rows = hidden.reshape(nblocks, sub_rows, feat_width)
    all_lists = lax.all_gather(kept_blocks, "vocab", axis=0, tiled=True)
    own_list = kept_blocks[0]
    own_count = kept_count[0]
    label_tab = labels.reshape(shards, nblocks, sub_rows)
    lse_tab = lse.reshape(shards, nblocks, sub_rows)
    scale_tab = loss_grad.reshape(shards, nblocks, sub_rows)
    vocab_ids = my_index * voc_rows + jnp.arange(voc_rows, dtype=jnp.int32)
    block_ids = jnp.arange(nblocks, dtype=jnp.int32)

    def block_terms(slot_index, block_rows):
        row_block = own_list[slot_index]
        picked_labels = lax.dynamic_index_in_dim(label_tab, row_block, 1, keepdims=False).reshape(
            RB
        )
        picked_lse = lax.dynamic_index_in_dim(lse_tab, row_block, 1, keepdims=False).reshape(RB)
        picked_scale = lax.dynamic_index_in_dim(scale_tab, row_block, 1, keepdims=False).reshape(RB)
        logits = lax.dot_general(
            block_rows, weight, (((1,), (1,)), ((), ())), preferred_element_type=jnp.float32
        )
        onehot = (picked_labels[:, None] == vocab_ids[None, :]).astype(jnp.float32)
        keep_slot = (slot_index < own_count).astype(jnp.float32)
        factor = picked_scale * keep_slot
        block_grad = (factor[:, None] * (jnp.exp(logits - picked_lse[:, None]) - onehot)).astype(
            jnp.bfloat16
        )
        hidden_part = jnp.dot(block_grad, weight, preferred_element_type=jnp.float32).astype(
            jnp.bfloat16
        )
        update = lax.dot_general(
            block_grad, block_rows, (((0,), (0,)), ((), ())), preferred_element_type=jnp.float32
        )
        return (hidden_part, update)

    zero_w = jnp.zeros((voc_rows, feat_width), jnp.float32)

    def slot_step(slot_index, carried):
        grad_w, grad_acc = carried
        column = lax.dynamic_index_in_dim(all_lists, slot_index, 1, keepdims=False)
        outgoing = local_rows[column].reshape(shards * sub_rows, feat_width)
        block_rows = lax.all_to_all(outgoing, "vocab", split_axis=0, concat_axis=0, tiled=True)
        hidden_part, update = block_terms(slot_index, block_rows)
        returned = lax.all_to_all(hidden_part, "vocab", split_axis=0, concat_axis=0, tiled=True)
        select = (block_ids[:, None] == column[None, :]).astype(jnp.bfloat16)
        grad_acc = grad_acc + jnp.dot(
            select,
            returned.reshape(shards, sub_rows * feat_width),
            preferred_element_type=jnp.float32,
        )
        return (grad_w + update, grad_acc)

    empty_acc = jnp.zeros((nblocks, sub_rows * feat_width), jnp.float32)
    grad_w, grad_h = lax.fori_loop(0, slot_count, slot_step, (zero_w, empty_acc))
    grad_hidden = grad_h.reshape(tok_rows, feat_width).astype(jnp.bfloat16)
    return (grad_hidden, grad_w.astype(jnp.bfloat16))


def solution(mesh):
    in_specs = (
        P(("groups", "vocab"), None),
        P("vocab", None),
        P("groups"),
        P("groups"),
        P("groups"),
        P(("groups", "vocab"), None),
        P(("groups", "vocab")),
    )
    out_specs = (P(("groups", "vocab"), None), P(("groups", "vocab"), None))
    return jax.shard_map(
        per_device, mesh=mesh, in_specs=in_specs, out_specs=out_specs, check_vma=False
    )
```

```python
import functools

import jax
import jax.numpy as jnp
from jax import lax
from jax.experimental import pallas as pl
from jax.experimental.pallas import tpu as pltpu
from jax.sharding import PartitionSpec as P

RB = 128
MESH = pl.DeviceIdType.MESH
VMEM_CAP = 60 * 1024 * 1024


def exchange_kernel(
    n, rows, chunks, sw,
    hid, w_hbm, lab, lse, scl, kept_blocks, kept_count,
    gh, gt_ref, x_hbm,
    lists, columns, g_ref, x_ref, w, gw, lists_buf, out_buf, in_buf, hbuf, ret, gret, gsum, part, sel, logits,
    w_sem, x_sem, l_send, l_recv, s1_send, s1_recv, s2_send, in_recv,
    r_send, ret_recv, gret_recv, gs_send, part_recv,
):
    half, quarter = n // 2, n // 4
    cw = 2 * sw
    me = lax.axis_index("vocab")
    q = lax.rem(me, quarter)
    side = lax.div(me, half)
    hb = side * half
    ob = half - hb
    ml = me - hb
    plane = lax.div(ml, quarter)
    gate_base = quarter + side * quarter
    gate_target = half - side * quarter + q
    is_gate = plane == 1 - side
    f32, bf16 = jnp.float32, jnp.bfloat16

    def remote(src, dst, send, recv, to):
        return pltpu.make_async_remote_copy(
            src_ref=src, dst_ref=dst, send_sem=send, recv_sem=recv,
            device_id={"vocab": to}, device_id_type=MESH,
        )

    def wait_for(ref, sem):
        pltpu.make_async_copy(ref, ref, sem).wait()

    def cols(c):
        return pl.ds(pl.multiple_of(c * cw, 128), cw)

    def subs(c, a):
        return pl.ds(pl.multiple_of(c * cw + a * sw, 128), sw)

    def peer(dd):
        return hb + lax.rem(ml + 1 + dd, half)

    def source(i):
        return ob + i * quarter + q

    sub = rows // kept_blocks.shape[1]
    row_at = lax.broadcasted_iota(jnp.int32, lists.shape, 0)
    lane_at = lax.broadcasted_iota(jnp.int32, lists.shape, 1)
    slot_at = lax.div(row_at, sub)
    source_row = lax.rem(row_at, sub)
    for k in range(kept_blocks.shape[1]):
        source_row += jnp.where(slot_at == k, kept_blocks[0, k] * sub, 0)
    lists[...] = source_row

    barrier = pltpu.get_barrier_semaphore()

    @pl.loop(1, n)
    def _(d):
        pl.semaphore_signal(
            barrier, inc=1, device_id={"vocab": lax.rem(me + d, n)}, device_id_type=MESH
        )

    pl.semaphore_wait(barrier, n - 1)

    def relay_copy(c):
        return remote(
            hid.at[:, cols(c)], gw.at[plane, c], s1_send.at[c], s1_recv.at[plane, c], gate_target
        )

    @pl.loop(0, half - 1)
    def _(dd):
        remote(lists, lists_buf.at[half - 2 - dd], l_send, l_recv, peer(dd)).start()

    pltpu.make_async_copy(lists, lists_buf.at[half - 1], l_recv).start()
    relay_copy(0).start()
    relay_copy(1).start()
    weight_copy = pltpu.make_async_copy(w_hbm, w, w_sem)
    weight_copy.start()
    mine = source_row == lane_at

    def column(table, mask):
        spread = jnp.where(mask[None], table[:, None, :], 0.0)
        return jnp.sum(spread, axis=-1, keepdims=True).reshape(n * rows, 1)

    columns[0] = column(lab[...].astype(f32), mine)
    columns[1] = column(lse[...], mine)
    columns[2] = column(scl[...], mine & (slot_at < kept_count[0]))
    wait_for(lists_buf, l_recv)
    wanted = lists_buf[...].reshape(half * rows, lists.shape[1])
    lane = lax.broadcasted_iota(jnp.int32, wanted.shape, 1)
    sel[...] = (wanted == lane).astype(f32).astype(bf16)

    def pack(value, count):
        v = value.reshape(count, rows, cw)
        return jnp.concatenate([v[:, :, :sw], v[:, :, sw:]], axis=1).astype(bf16)

    def unpack(value, count):
        v = value.astype(f32)
        parts = [v[:, a * rows : (a + 1) * rows, :].reshape(count * rows, sw) for a in range(2)]
        return [p.astype(bf16) for p in parts]

    def send_rows(c, kind, block, owner):
        picked = jnp.dot(sel[...], block, preferred_element_type=f32)
        out_buf[c, kind] = pack(picked, half)

        @pl.loop(0, half - 1)
        def _(dd):
            remote(
                out_buf.at[c, kind, dd], in_buf.at[c, owner],
                s2_send.at[c, kind], in_recv.at[c], peer(dd),
            ).start()

        pltpu.make_async_copy(
            out_buf.at[c, kind, half - 1], in_buf.at[c, owner], in_recv.at[c]
        ).start()

    def logits_step(c):
        wait_for(in_buf.at[c], in_recv.at[c])
        x0, x1 = unpack(in_buf[c], n)
        x_ref[:, subs(c, 0)] = x0
        x_ref[:, subs(c, 1)] = x1
        dims = (((1,), (1,)), ((), ()))
        logits[...] += lax.dot_general(
            x_ref[:, cols(c)], w[:, cols(c)], dims, preferred_element_type=f32
        )

    logits[...] = jnp.zeros_like(logits)
    weight_copy.wait()
    lag = 2

    @pl.loop(0, chunks + lag)
    def _(c):
        @pl.when(c + 2 < chunks)
        def _():
            relay_copy(c + 2).start()

        @pl.when(c < chunks)
        def _():
            send_rows(c, 0, hid[:, cols(c)], me)

            @pl.when(is_gate)
            def _():
                @pl.loop(0, 2)
                def _(i):
                    wait_for(gw.at[i, c], s1_recv.at[i, c])
                    send_rows(c, 1 + i, gw[i, c], source(i))

        @pl.when(c >= lag)
        def _():
            logits_step(c - lag)

    ids = lax.broadcasted_iota(jnp.int32, logits.shape, 1) + me * logits.shape[1]
    onehot = (columns[0] == ids.astype(f32)).astype(f32)
    scale = columns[2]
    grad = scale * (jnp.exp(logits[...] - columns[1]) - onehot)
    g_ref[...] = jnp.where(scale != 0, grad, 0.0).astype(bf16)
    x_copy = pltpu.make_async_copy(x_ref, x_hbm, x_sem)
    x_copy.start()

    def gather_sum(values):
        y = jnp.concatenate(unpack(values, half), axis=1)
        return lax.dot_general(
            sel[...], y, (((0,), (0,)), ((), ())), preferred_element_type=f32
        )

    @pl.loop(0, chunks + 2 * lag)
    def _(c):
        @pl.when(c < chunks)
        def _():
            hp = jnp.dot(g_ref[...], w[:, cols(c)], preferred_element_type=f32)
            hbuf[c] = pack(hp, n)

            def far(i, off):
                qq = lax.rem(q + off, quarter)
                gate = gate_base + qq
                d = lax.rem(ml - (gate - hb) - 1 + half, half)
                return remote(
                    hbuf.at[c, ob + i * quarter + qq], gret.at[c, i, d],
                    r_send.at[c], gret_recv.at[c, i], gate,
                )

            @pl.loop(0, 2)
            def _(i):
                @pl.loop(1, quarter)
                def _(off):
                    far(i, off).start()

                @pl.when(is_gate)
                def _():
                    pltpu.make_async_copy(
                        hbuf.at[c, source(i)], gret.at[c, i, half - 1], gret_recv.at[c, i]
                    ).start()

                @pl.when(jnp.logical_not(is_gate))
                def _():
                    far(i, 0).start()

            @pl.loop(0, half - 1)
            def _(dd):
                remote(
                    hbuf.at[c, peer(dd)], ret.at[c, half - 2 - dd],
                    r_send.at[c], ret_recv.at[c], peer(dd),
                ).start()

            pltpu.make_async_copy(hbuf.at[c, me], ret.at[c, half - 1], ret_recv.at[c]).start()

        @pl.when(c == 1)
        def _():
            gt_ref[...] = jnp.transpose(g_ref[...].astype(f32)).astype(bf16)

        @pl.when((c >= lag) & (c < chunks + lag) & is_gate)
        def _():
            k = c - lag

            @pl.loop(0, 2)
            def _(i):
                wait_for(gret.at[k, i], gret_recv.at[k, i])
                gsum[k, i] = gather_sum(gret[k, i]).astype(bf16)
                remote(
                    gsum.at[k, i], part.at[k], gs_send.at[k, i], part_recv.at[k], source(i)
                ).start()

        @pl.when(c >= 2 * lag)
        def _():
            k = c - 2 * lag
            wait_for(ret.at[k], ret_recv.at[k])
            near = gather_sum(ret[k])
            wait_for(part.at[k], part_recv.at[k])
            gh[:, cols(k)] = (near + part[k].astype(f32)).astype(bf16)

    x_copy.wait()
    wait_for(lists_buf.at[pl.ds(0, half - 1)], l_send)

    @pl.loop(0, chunks)
    def _(c):
        wait_for(gw.at[0, c], s1_send.at[c])
        wait_for(out_buf.at[c, 0, pl.ds(0, half - 1)], s2_send.at[c, 0])

        @pl.when(is_gate)
        def _():
            @pl.loop(0, 2)
            def _(i):
                wait_for(out_buf.at[c, 1 + i, pl.ds(0, half - 1)], s2_send.at[c, 1 + i])
                wait_for(gsum.at[c, i], gs_send.at[c, i])

            wait_for(hbuf.at[c, pl.ds(0, half + 2 * quarter - 3)], r_send.at[c])

        @pl.when(jnp.logical_not(is_gate))
        def _():
            wait_for(hbuf.at[c, pl.ds(0, half + 2 * quarter - 1)], r_send.at[c])


def scratch_of(n, rows, chunks, sw, toks, voc, width):
    half = n // 2
    bf16 = jnp.bfloat16
    dma = pltpu.SemaphoreType.DMA
    return [
        pltpu.VMEM((rows, toks), jnp.int32),
        pltpu.VMEM((3, n * rows, 1), jnp.float32),
        pltpu.VMEM((n * rows, voc), bf16),
        pltpu.VMEM((n * rows, width), bf16),
        pltpu.VMEM((voc, width), bf16),
        pltpu.VMEM((2, chunks, toks, 2 * sw), bf16),
        pltpu.VMEM((half, rows, toks), jnp.int32),
        pltpu.VMEM((chunks, 3, half, 2 * rows, sw), bf16),
        pltpu.VMEM((chunks, n, 2 * rows, sw), bf16),
        pltpu.VMEM((chunks, n, 2 * rows, sw), bf16),
        pltpu.VMEM((chunks, half, 2 * rows, sw), bf16),
        pltpu.VMEM((chunks, 2, half, 2 * rows, sw), bf16),
        pltpu.VMEM((chunks, 2, toks, 2 * sw), bf16),
        pltpu.VMEM((chunks, toks, 2 * sw), bf16),
        pltpu.VMEM((half * rows, toks), bf16),
        pltpu.VMEM((n * rows, voc), jnp.float32),
        dma, dma, dma, dma,
        dma((chunks,)), dma((2, chunks)), dma((chunks, 3)), dma((chunks,)),
        dma((chunks,)), dma((chunks,)), dma((chunks, 2)), dma((chunks, 2)), dma((chunks,)),
    ]


def plan(n, tok_rows, voc, width, slots):
    rows = slots * (RB // n)
    if n % 4 or rows % 8 or tok_rows != 128 or width % 256:
        return None
    pairs = width // 256
    chunks = min([c for c in range(1, pairs + 1) if pairs % c == 0], key=lambda c: abs(c - 7))
    need = 2 * voc * width + 4 * n * rows * voc + 2 * n * rows * voc
    need += 2 * width * (n * rows * 6 + tok_rows * 7)
    if need > VMEM_CAP - 3 * 1024 * 1024:
        return None
    return rows, chunks, width // chunks // 2


def per_device(hidden, weight, lse, loss_grad, labels, kept_blocks, kept_count):
    n = lax.axis_size("vocab")
    tok_rows, width = hidden.shape
    voc = weight.shape[0]
    slots = kept_blocks.shape[1]
    planned = plan(n, tok_rows, voc, width, slots)
    if planned is None:
        return by_slots(hidden, weight, lse, loss_grad, labels, kept_blocks, kept_count)
    rows, chunks, sw = planned
    vmem = pl.BlockSpec(memory_space=pltpu.VMEM)
    smem = pl.BlockSpec(memory_space=pltpu.SMEM)
    hbm = pl.BlockSpec(memory_space=pl.ANY)
    tables = [t.reshape(n, tok_rows) for t in (labels, lse, loss_grad)]
    grad_h, gt, x = pl.pallas_call(
        functools.partial(exchange_kernel, n, rows, chunks, sw),
        out_shape=(
            jax.ShapeDtypeStruct((tok_rows, width), jnp.bfloat16),
            jax.ShapeDtypeStruct((voc, n * rows), jnp.bfloat16),
            jax.ShapeDtypeStruct((n * rows, width), jnp.bfloat16),
        ),
        in_specs=[vmem, hbm, vmem, vmem, vmem, smem, smem],
        out_specs=(vmem, vmem, hbm),
        scratch_shapes=scratch_of(n, rows, chunks, sw, tok_rows, voc, width),
        compiler_params=pltpu.CompilerParams(
            collective_id=0, has_side_effects=True, vmem_limit_bytes=VMEM_CAP
        ),
        name="exchange",
    )(hidden, weight, *tables, kept_blocks, kept_count)
    return grad_h, weight_gradient(gt, x, 2 * sw)


def weight_gradient(gt, x, cw):
    voc, depth = gt.shape
    width = x.shape[1]
    step = 256

    def kernel(gt_ref, x_ref, out_ref):
        for at in range(0, voc, step):
            out_ref[at : at + step, :] = jnp.dot(
                gt_ref[at : at + step, :], x_ref[...], preferred_element_type=jnp.float32
            ).astype(jnp.bfloat16)

    return pl.pallas_call(
        kernel,
        out_shape=jax.ShapeDtypeStruct((voc, width), jnp.bfloat16),
        grid=(width // cw,),
        in_specs=[
            pl.BlockSpec((voc, depth), lambda i: (0, 0)),
            pl.BlockSpec((depth, cw), lambda i: (0, i)),
        ],
        out_specs=pl.BlockSpec((voc, cw), lambda i: (0, i)),
        cost_estimate=pl.CostEstimate(
            flops=2 * voc * depth * width,
            bytes_accessed=2 * (voc * depth + depth * width + voc * width),
            transcendentals=0,
        ),
        compiler_params=pltpu.CompilerParams(vmem_limit_bytes=32 * 1024 * 1024),
        name="weight_gradient",
    )(gt, x)


def by_slots(hidden, weight, lse, loss_grad, labels, kept_blocks, kept_count):
    shards = lax.axis_size("vocab")
    my_index = lax.axis_index("vocab")
    tok_rows, feat_width = hidden.shape
    voc_rows = weight.shape[0]
    slot_count = kept_blocks.shape[1]
    sub_rows = RB // shards
    nblocks = tok_rows // sub_rows
    local_rows = hidden.reshape(nblocks, sub_rows, feat_width)
    all_lists = lax.all_gather(kept_blocks, "vocab", axis=0, tiled=True)
    own_list = kept_blocks[0]
    own_count = kept_count[0]
    label_tab = labels.reshape(shards, nblocks, sub_rows)
    lse_tab = lse.reshape(shards, nblocks, sub_rows)
    scale_tab = loss_grad.reshape(shards, nblocks, sub_rows)
    vocab_ids = my_index * voc_rows + jnp.arange(voc_rows, dtype=jnp.int32)
    block_ids = jnp.arange(nblocks, dtype=jnp.int32)

    def block_terms(slot_index, block_rows):
        row_block = own_list[slot_index]
        picked_labels = lax.dynamic_index_in_dim(label_tab, row_block, 1, keepdims=False).reshape(
            RB
        )
        picked_lse = lax.dynamic_index_in_dim(lse_tab, row_block, 1, keepdims=False).reshape(RB)
        picked_scale = lax.dynamic_index_in_dim(scale_tab, row_block, 1, keepdims=False).reshape(RB)
        logits = lax.dot_general(
            block_rows, weight, (((1,), (1,)), ((), ())), preferred_element_type=jnp.float32
        )
        onehot = (picked_labels[:, None] == vocab_ids[None, :]).astype(jnp.float32)
        keep_slot = (slot_index < own_count).astype(jnp.float32)
        factor = picked_scale * keep_slot
        block_grad = (factor[:, None] * (jnp.exp(logits - picked_lse[:, None]) - onehot)).astype(
            jnp.bfloat16
        )
        hidden_part = jnp.dot(block_grad, weight, preferred_element_type=jnp.float32).astype(
            jnp.bfloat16
        )
        update = lax.dot_general(
            block_grad, block_rows, (((0,), (0,)), ((), ())), preferred_element_type=jnp.float32
        )
        return (hidden_part, update)

    zero_w = jnp.zeros((voc_rows, feat_width), jnp.float32)

    def slot_step(slot_index, carried):
        grad_w, grad_acc = carried
        column = lax.dynamic_index_in_dim(all_lists, slot_index, 1, keepdims=False)
        outgoing = local_rows[column].reshape(shards * sub_rows, feat_width)
        block_rows = lax.all_to_all(outgoing, "vocab", split_axis=0, concat_axis=0, tiled=True)
        hidden_part, update = block_terms(slot_index, block_rows)
        returned = lax.all_to_all(hidden_part, "vocab", split_axis=0, concat_axis=0, tiled=True)
        select = (block_ids[:, None] == column[None, :]).astype(jnp.bfloat16)
        grad_acc = grad_acc + jnp.dot(
            select,
            returned.reshape(shards, sub_rows * feat_width),
            preferred_element_type=jnp.float32,
        )
        return (grad_w + update, grad_acc)

    empty_acc = jnp.zeros((nblocks, sub_rows * feat_width), jnp.float32)
    grad_w, grad_h = lax.fori_loop(0, slot_count, slot_step, (zero_w, empty_acc))
    grad_hidden = grad_h.reshape(tok_rows, feat_width).astype(jnp.bfloat16)
    return (grad_hidden, grad_w.astype(jnp.bfloat16))


def solution(mesh):
    in_specs = (
        P(("groups", "vocab"), None),
        P("vocab", None),
        P("groups"),
        P("groups"),
        P("groups"),
        P(("groups", "vocab"), None),
        P(("groups", "vocab")),
    )
    out_specs = (P(("groups", "vocab"), None), P(("groups", "vocab"), None))
    return jax.shard_map(
        per_device, mesh=mesh, in_specs=in_specs, out_specs=out_specs, check_vma=False
    )
```

```python
import functools

import jax
import jax.numpy as jnp
from jax import lax
from jax.experimental import pallas as pl
from jax.experimental.pallas import tpu as pltpu
from jax.sharding import PartitionSpec as P

RB = 128
MESH = pl.DeviceIdType.MESH
VMEM_CAP = 60 * 1024 * 1024


def exchange_kernel(
    n, rows, chunks, sw,
    hid, w_hbm, lab, lse, scl, kept_blocks, kept_count,
    gh, gt_ref, x_hbm,
    lists, columns, g_ref, x_ref, w, gw, lists_buf, out_buf, in_buf, hbuf, ret, gret, gsum, part, sel, logits,
    w_sem, x_sem, l_send, l_recv, s1_send, s1_recv, s2_send, in_recv,
    r_send, ret_recv, gret_recv, gs_send, part_recv,
):
    half, quarter = n // 2, n // 4
    cw = 2 * sw
    me = lax.axis_index("vocab")
    q = lax.rem(me, quarter)
    side = lax.div(me, half)
    hb = side * half
    ob = half - hb
    ml = me - hb
    plane = lax.div(ml, quarter)
    gate_base = quarter + side * quarter
    gate_target = half - side * quarter + q
    is_gate = plane == 1 - side
    f32, bf16 = jnp.float32, jnp.bfloat16

    def remote(src, dst, send, recv, to):
        return pltpu.make_async_remote_copy(
            src_ref=src, dst_ref=dst, send_sem=send, recv_sem=recv,
            device_id={"vocab": to}, device_id_type=MESH,
        )

    def wait_for(ref, sem):
        pltpu.make_async_copy(ref, ref, sem).wait()

    def cols(c):
        return pl.ds(pl.multiple_of(c * cw, 128), cw)

    def subs(c, a):
        return pl.ds(pl.multiple_of(c * cw + a * sw, 128), sw)

    def peer(dd):
        return hb + lax.rem(ml + 1 + dd, half)

    def source(i):
        return ob + i * quarter + q

    sub = rows // kept_blocks.shape[1]
    row_at = lax.broadcasted_iota(jnp.int32, lists.shape, 0)
    lane_at = lax.broadcasted_iota(jnp.int32, lists.shape, 1)
    slot_at = lax.div(row_at, sub)
    source_row = lax.rem(row_at, sub)
    for k in range(kept_blocks.shape[1]):
        source_row += jnp.where(slot_at == k, kept_blocks[0, k] * sub, 0)
    lists[...] = source_row

    weight_copy = pltpu.make_async_copy(w_hbm, w, w_sem)
    weight_copy.start()

    barrier = pltpu.get_barrier_semaphore()

    @pl.loop(1, n)
    def _(d):
        pl.semaphore_signal(
            barrier, inc=1, device_id={"vocab": lax.rem(me + d, n)}, device_id_type=MESH
        )

    pl.semaphore_wait(barrier, n - 1)

    ahead, pieces = 1, 8
    piece_rows = hid.shape[0] // pieces

    def relay_copy(c, piece):
        at = pl.ds(pl.multiple_of(piece * piece_rows, 16), piece_rows)
        return remote(
            hid.at[at, cols(c)], gw.at[plane, c, at],
            s1_send.at[c], s1_recv.at[plane, c], gate_target,
        )

    @pl.loop(0, half - 1)
    def _(dd):
        remote(lists, lists_buf.at[half - 2 - dd], l_send, l_recv, peer(dd)).start()

    pltpu.make_async_copy(lists, lists_buf.at[half - 1], l_recv).start()
    for c in range(1):
        for piece in range(8):
            relay_copy(c, piece).start()
    mine = source_row == lane_at

    def column(table, mask):
        spread = jnp.where(mask[None], table[:, None, :], 0.0)
        return jnp.sum(spread, axis=-1, keepdims=True).reshape(n * rows, 1)

    columns[0] = column(lab[...].astype(f32), mine)
    columns[1] = column(lse[...], mine)
    columns[2] = column(scl[...], mine & (slot_at < kept_count[0]))
    wait_for(lists_buf, l_recv)
    wanted = lists_buf[...].reshape(half * rows, lists.shape[1])
    lane = lax.broadcasted_iota(jnp.int32, wanted.shape, 1)
    sel[...] = (wanted == lane).astype(f32).astype(bf16)

    def pack(value, count):
        v = value.reshape(count, rows, cw)
        return jnp.concatenate([v[:, :, :sw], v[:, :, sw:]], axis=1).astype(bf16)

    def unpack(value, count):
        v = value.astype(f32)
        parts = [v[:, a * rows : (a + 1) * rows, :].reshape(count * rows, sw) for a in range(2)]
        return [p.astype(bf16) for p in parts]

    def relay_piece(c, dd):
        every = half // pieces

        @pl.when((c < chunks) & (lax.rem(dd + 1, every) == 0))
        def _():
            relay_copy(c, lax.div(dd, every)).start()

    def send_rows(c, kind, block, owner, kind_is_own):
        picked = jnp.dot(sel[...], block, preferred_element_type=f32)
        out_buf[c, kind] = pack(picked, half)

        @pl.loop(0, half - 1)
        def _(dd):
            remote(
                out_buf.at[c, kind, dd], in_buf.at[c, owner],
                s2_send.at[c, kind], in_recv.at[c], peer(dd),
            ).start()
            if kind_is_own:
                relay_piece(c + ahead, dd)

        if kind_is_own:
            relay_piece(c + ahead, half - 1)
        pltpu.make_async_copy(
            out_buf.at[c, kind, half - 1], in_buf.at[c, owner], in_recv.at[c]
        ).start()

    def logits_step(c):
        wait_for(in_buf.at[c], in_recv.at[c])
        x0, x1 = unpack(in_buf[c], n)
        x_ref[:, subs(c, 0)] = x0
        x_ref[:, subs(c, 1)] = x1
        dims = (((1,), (1,)), ((), ()))
        logits[...] += lax.dot_general(
            x_ref[:, cols(c)], w[:, cols(c)], dims, preferred_element_type=f32
        )

    logits[...] = jnp.zeros_like(logits)
    lag = 2

    @pl.loop(0, chunks + lag)
    def _(c):
        @pl.when(c < chunks)
        def _():
            send_rows(c, 0, hid[:, cols(c)], me, True)

            @pl.when(is_gate)
            def _():
                @pl.loop(0, 2)
                def _(i):
                    wait_for(gw.at[i, c], s1_recv.at[i, c])
                    send_rows(c, 1 + i, gw[i, c], source(i), False)

        @pl.when(c == lag)
        def _():
            weight_copy.wait()

        @pl.when(c >= lag)
        def _():
            logits_step(c - lag)

    ids = lax.broadcasted_iota(jnp.int32, logits.shape, 1) + me * logits.shape[1]
    onehot = (columns[0] == ids.astype(f32)).astype(f32)
    scale = columns[2]
    grad = scale * (jnp.exp(logits[...] - columns[1]) - onehot)
    g_ref[...] = jnp.where(scale != 0, grad, 0.0).astype(bf16)
    x_copy = pltpu.make_async_copy(x_ref, x_hbm, x_sem)
    x_copy.start()

    def gather_sum(values):
        y = jnp.concatenate(unpack(values, half), axis=1)
        return lax.dot_general(
            sel[...], y, (((0,), (0,)), ((), ())), preferred_element_type=f32
        )

    @pl.loop(0, chunks + 2 * lag)
    def _(c):
        @pl.when(c < chunks)
        def _():
            hp = jnp.dot(g_ref[...], w[:, cols(c)], preferred_element_type=f32)
            hbuf[c] = pack(hp, n)

            def far(i, off):
                qq = lax.rem(q + off, quarter)
                gate = gate_base + qq
                d = lax.rem(ml - (gate - hb) - 1 + half, half)
                return remote(
                    hbuf.at[c, ob + i * quarter + qq], gret.at[c, i, d],
                    r_send.at[c], gret_recv.at[c, i], gate,
                )

            @pl.loop(0, 2)
            def _(i):
                @pl.loop(1, quarter)
                def _(off):
                    far(i, off).start()

                @pl.when(is_gate)
                def _():
                    pltpu.make_async_copy(
                        hbuf.at[c, source(i)], gret.at[c, i, half - 1], gret_recv.at[c, i]
                    ).start()

                @pl.when(jnp.logical_not(is_gate))
                def _():
                    far(i, 0).start()

            @pl.loop(0, half - 1)
            def _(dd):
                remote(
                    hbuf.at[c, peer(dd)], ret.at[c, half - 2 - dd],
                    r_send.at[c], ret_recv.at[c], peer(dd),
                ).start()

            pltpu.make_async_copy(hbuf.at[c, me], ret.at[c, half - 1], ret_recv.at[c]).start()

        @pl.when(c == 1)
        def _():
            gt_ref[...] = jnp.transpose(g_ref[...].astype(f32)).astype(bf16)

        @pl.when((c >= lag) & (c < chunks + lag) & is_gate)
        def _():
            k = c - lag

            @pl.loop(0, 2)
            def _(i):
                wait_for(gret.at[k, i], gret_recv.at[k, i])
                gsum[k, i] = gather_sum(gret[k, i]).astype(bf16)
                remote(
                    gsum.at[k, i], part.at[k], gs_send.at[k, i], part_recv.at[k], source(i)
                ).start()

        @pl.when(c >= 2 * lag)
        def _():
            k = c - 2 * lag
            wait_for(ret.at[k], ret_recv.at[k])
            near = gather_sum(ret[k])
            wait_for(part.at[k], part_recv.at[k])
            gh[:, cols(k)] = (near + part[k].astype(f32)).astype(bf16)

    x_copy.wait()
    wait_for(lists_buf.at[pl.ds(0, half - 1)], l_send)

    @pl.loop(0, chunks)
    def _(c):
        wait_for(gw.at[0, c], s1_send.at[c])
        wait_for(out_buf.at[c, 0, pl.ds(0, half - 1)], s2_send.at[c, 0])

        @pl.when(is_gate)
        def _():
            @pl.loop(0, 2)
            def _(i):
                wait_for(out_buf.at[c, 1 + i, pl.ds(0, half - 1)], s2_send.at[c, 1 + i])
                wait_for(gsum.at[c, i], gs_send.at[c, i])

            wait_for(hbuf.at[c, pl.ds(0, half + 2 * quarter - 3)], r_send.at[c])

        @pl.when(jnp.logical_not(is_gate))
        def _():
            wait_for(hbuf.at[c, pl.ds(0, half + 2 * quarter - 1)], r_send.at[c])


def scratch_of(n, rows, chunks, sw, toks, voc, width):
    half = n // 2
    bf16 = jnp.bfloat16
    dma = pltpu.SemaphoreType.DMA
    return [
        pltpu.VMEM((rows, toks), jnp.int32),
        pltpu.VMEM((3, n * rows, 1), jnp.float32),
        pltpu.VMEM((n * rows, voc), bf16),
        pltpu.VMEM((n * rows, width), bf16),
        pltpu.VMEM((voc, width), bf16),
        pltpu.VMEM((2, chunks, toks, 2 * sw), bf16),
        pltpu.VMEM((half, rows, toks), jnp.int32),
        pltpu.VMEM((chunks, 3, half, 2 * rows, sw), bf16),
        pltpu.VMEM((chunks, n, 2 * rows, sw), bf16),
        pltpu.VMEM((chunks, n, 2 * rows, sw), bf16),
        pltpu.VMEM((chunks, half, 2 * rows, sw), bf16),
        pltpu.VMEM((chunks, 2, half, 2 * rows, sw), bf16),
        pltpu.VMEM((chunks, 2, toks, 2 * sw), bf16),
        pltpu.VMEM((chunks, toks, 2 * sw), bf16),
        pltpu.VMEM((half * rows, toks), bf16),
        pltpu.VMEM((n * rows, voc), jnp.float32),
        dma, dma, dma, dma,
        dma((chunks,)), dma((2, chunks)), dma((chunks, 3)), dma((chunks,)),
        dma((chunks,)), dma((chunks,)), dma((chunks, 2)), dma((chunks, 2)), dma((chunks,)),
    ]


def plan(n, tok_rows, voc, width, slots):
    rows = slots * (RB // n)
    if n % 16 or rows % 8 or tok_rows != 128 or width % 256 or voc % 256:
        return None
    pairs = width // 256
    chunks = min([c for c in range(1, pairs + 1) if pairs % c == 0], key=lambda c: abs(c - 7))
    need = 2 * voc * width + 4 * n * rows * voc + 2 * n * rows * voc
    need += 2 * width * (n * rows * 6 + tok_rows * 7)
    if need > VMEM_CAP - 3 * 1024 * 1024:
        return None
    return rows, chunks, width // chunks // 2


def per_device(hidden, weight, lse, loss_grad, labels, kept_blocks, kept_count):
    n = lax.axis_size("vocab")
    tok_rows, width = hidden.shape
    voc = weight.shape[0]
    slots = kept_blocks.shape[1]
    planned = plan(n, tok_rows, voc, width, slots)
    if planned is None:
        return by_slots(hidden, weight, lse, loss_grad, labels, kept_blocks, kept_count)
    rows, chunks, sw = planned
    vmem = pl.BlockSpec(memory_space=pltpu.VMEM)
    smem = pl.BlockSpec(memory_space=pltpu.SMEM)
    hbm = pl.BlockSpec(memory_space=pl.ANY)
    tables = [t.reshape(n, tok_rows) for t in (labels, lse, loss_grad)]
    grad_h, gt, x = pl.pallas_call(
        functools.partial(exchange_kernel, n, rows, chunks, sw),
        out_shape=(
            jax.ShapeDtypeStruct((tok_rows, width), jnp.bfloat16),
            jax.ShapeDtypeStruct((voc, n * rows), jnp.bfloat16),
            jax.ShapeDtypeStruct((n * rows, width), jnp.bfloat16),
        ),
        in_specs=[vmem, hbm, vmem, vmem, vmem, smem, smem],
        out_specs=(vmem, vmem, hbm),
        scratch_shapes=scratch_of(n, rows, chunks, sw, tok_rows, voc, width),
        compiler_params=pltpu.CompilerParams(
            collective_id=0, has_side_effects=True, vmem_limit_bytes=VMEM_CAP
        ),
        name="exchange",
    )(hidden, weight, *tables, kept_blocks, kept_count)
    return grad_h, weight_gradient(gt, x, 2 * sw)


def weight_gradient(gt, x, cw):
    voc, depth = gt.shape
    width = x.shape[1]
    steps, split = width // cw, 4
    band = voc // split

    def kernel(gt_hbm, x_hbm, out_hbm, gt_ref, x_ref, out_ref, gt_sem, in_sem, out_sem):
        gt_copy = pltpu.make_async_copy(gt_hbm, gt_ref, gt_sem)
        gt_copy.start()

        def span(i):
            return pl.ds(i * cw, cw)

        def load(i):
            return pltpu.make_async_copy(x_hbm.at[:, span(i)], x_ref.at[:, span(i)], in_sem.at[i])

        def store(i, r):
            at = pl.ds(r * band, band)
            return pltpu.make_async_copy(
                out_ref.at[at, span(i)], out_hbm.at[at, span(i)], out_sem.at[i, r]
            )

        for i in range(steps):
            load(i).start()
        gt_copy.wait()
        for i in range(steps):
            load(i).wait()
            for r in range(split):
                at = pl.ds(r * band, band)
                out_ref[at, span(i)] = jnp.dot(
                    gt_ref[at, :], x_ref[:, span(i)], preferred_element_type=jnp.float32
                ).astype(jnp.bfloat16)
                store(i, r).start()
        for i in range(steps):
            for r in range(split):
                store(i, r).wait()

    hbm = pl.BlockSpec(memory_space=pl.ANY)
    dma = pltpu.SemaphoreType.DMA
    return pl.pallas_call(
        kernel,
        out_shape=jax.ShapeDtypeStruct((voc, width), jnp.bfloat16),
        in_specs=[hbm, hbm],
        out_specs=hbm,
        scratch_shapes=[
            pltpu.VMEM((voc, depth), jnp.bfloat16),
            pltpu.VMEM((depth, width), jnp.bfloat16),
            pltpu.VMEM((voc, width), jnp.bfloat16),
            dma, dma((steps,)), dma((steps, split)),
        ],
        cost_estimate=pl.CostEstimate(
            flops=2 * voc * depth * width,
            bytes_accessed=2 * (voc * depth + depth * width + voc * width),
            transcendentals=0,
        ),
        compiler_params=pltpu.CompilerParams(vmem_limit_bytes=VMEM_CAP),
        name="weight_gradient",
    )(gt, x)


def by_slots(hidden, weight, lse, loss_grad, labels, kept_blocks, kept_count):
    shards = lax.axis_size("vocab")
    my_index = lax.axis_index("vocab")
    tok_rows, feat_width = hidden.shape
    voc_rows = weight.shape[0]
    slot_count = kept_blocks.shape[1]
    sub_rows = RB // shards
    nblocks = tok_rows // sub_rows
    local_rows = hidden.reshape(nblocks, sub_rows, feat_width)
    all_lists = lax.all_gather(kept_blocks, "vocab", axis=0, tiled=True)
    own_list = kept_blocks[0]
    own_count = kept_count[0]
    label_tab = labels.reshape(shards, nblocks, sub_rows)
    lse_tab = lse.reshape(shards, nblocks, sub_rows)
    scale_tab = loss_grad.reshape(shards, nblocks, sub_rows)
    vocab_ids = my_index * voc_rows + jnp.arange(voc_rows, dtype=jnp.int32)
    block_ids = jnp.arange(nblocks, dtype=jnp.int32)

    def block_terms(slot_index, block_rows):
        row_block = own_list[slot_index]
        picked_labels = lax.dynamic_index_in_dim(label_tab, row_block, 1, keepdims=False).reshape(
            RB
        )
        picked_lse = lax.dynamic_index_in_dim(lse_tab, row_block, 1, keepdims=False).reshape(RB)
        picked_scale = lax.dynamic_index_in_dim(scale_tab, row_block, 1, keepdims=False).reshape(RB)
        logits = lax.dot_general(
            block_rows, weight, (((1,), (1,)), ((), ())), preferred_element_type=jnp.float32
        )
        onehot = (picked_labels[:, None] == vocab_ids[None, :]).astype(jnp.float32)
        keep_slot = (slot_index < own_count).astype(jnp.float32)
        factor = picked_scale * keep_slot
        block_grad = (factor[:, None] * (jnp.exp(logits - picked_lse[:, None]) - onehot)).astype(
            jnp.bfloat16
        )
        hidden_part = jnp.dot(block_grad, weight, preferred_element_type=jnp.float32).astype(
            jnp.bfloat16
        )
        update = lax.dot_general(
            block_grad, block_rows, (((0,), (0,)), ((), ())), preferred_element_type=jnp.float32
        )
        return (hidden_part, update)

    zero_w = jnp.zeros((voc_rows, feat_width), jnp.float32)

    def slot_step(slot_index, carried):
        grad_w, grad_acc = carried
        column = lax.dynamic_index_in_dim(all_lists, slot_index, 1, keepdims=False)
        outgoing = local_rows[column].reshape(shards * sub_rows, feat_width)
        block_rows = lax.all_to_all(outgoing, "vocab", split_axis=0, concat_axis=0, tiled=True)
        hidden_part, update = block_terms(slot_index, block_rows)
        returned = lax.all_to_all(hidden_part, "vocab", split_axis=0, concat_axis=0, tiled=True)
        select = (block_ids[:, None] == column[None, :]).astype(jnp.bfloat16)
        grad_acc = grad_acc + jnp.dot(
            select,
            returned.reshape(shards, sub_rows * feat_width),
            preferred_element_type=jnp.float32,
        )
        return (grad_w + update, grad_acc)

    empty_acc = jnp.zeros((nblocks, sub_rows * feat_width), jnp.float32)
    grad_w, grad_h = lax.fori_loop(0, slot_count, slot_step, (zero_w, empty_acc))
    grad_hidden = grad_h.reshape(tok_rows, feat_width).astype(jnp.bfloat16)
    return (grad_hidden, grad_w.astype(jnp.bfloat16))


def solution(mesh):
    in_specs = (
        P(("groups", "vocab"), None),
        P("vocab", None),
        P("groups"),
        P("groups"),
        P("groups"),
        P(("groups", "vocab"), None),
        P(("groups", "vocab")),
    )
    out_specs = (P(("groups", "vocab"), None), P(("groups", "vocab"), None))
    return jax.shard_map(
        per_device, mesh=mesh, in_specs=in_specs, out_specs=out_specs, check_vma=False
    )
```
